256 devices in a mesh: dom: 64 (over z, x, core), feat: 4 (over y).
Axes of the slice: x: 4, y: 4, z: 8, core: 2. Of those that a mesh axis runs over, the one named last changes fastest.
Arguments:
- initial: bfloat16 [131072, 256], P('dom', 'feat'), may hold values from -6 to 6
- history: bfloat16 [2, 131072, 256], P(None, 'dom', 'feat'), may hold values from -6 to 6
- adjacency: bfloat16 [131072, 2560], P('dom'), may hold values from 0 to 3, as said below
- tile_mask: int32 [1024, 20], P('dom'), may hold values from 0 to 1
- send_lists: int32 [64, 64, 8], P('dom'), may hold values from 0 to 2047
- weights: bfloat16 [3, 256, 256], P(None, 'feat'), may hold values from -0.375 to 0.375
Outputs:
- embeddings: bfloat16 [131072, 256], P('dom', 'feat')
The draws below stay inside these ranges and needn't reach their ends.
Inputs may be any that keep to these rules, and one draw needn't show every extreme that they name: adjacency entries are nonnegative.
All inputs are finite; a program needn't handle non-finite values.
Results may differ from the reference program's by a relative error of at most 0.0059.
Values may be sent and summed in bfloat16 or wider, within the bound.
No kernel may reach another device: no remote copies, remote signals or barrier semaphores. Data moves between devices by JAX's collectives and lax.ppermute only.
A program may use at most 64 MiB of HBM per device.

```python
import jax
import jax.numpy as jnp
from jax import lax

H = 256
ROWS = 2048
HALO = 512
LAYERS = 3
TILE = 128
SLOT = 8
NODES = 131072
N_DOM = 64


def draw_adjacency(key, part):
    key = jax.random.fold_in(key, 11)
    first, second = jax.random.split(key)
    edges = (jax.random.randint(first, (NODES, ROWS + HALO), 0, 32) == 0).astype(jnp.float32)
    values = jax.random.uniform(second, (NODES, ROWS + HALO), jnp.float32, 0.5, 1.5)
    return (edges * values).astype(jnp.bfloat16)


def draw_tile_mask(key, part):
    key = jax.random.fold_in(key, 23)
    blocks = NODES // TILE
    levels = jax.random.randint(key, (blocks, (ROWS + HALO) // TILE), 0, 100)
    rising = 20 + 70 * jnp.arange(blocks, dtype=jnp.int32) // max(blocks - 1, 1)
    return (levels < rising[:, None]).astype(jnp.int32)


def set_ends(entries, own_key, low, largest):
    spot = [jax.random.randint(jax.random.fold_in(own_key, axis), (), 0, length) for axis, length in enumerate(entries.shape)]
    widest = entries.shape.index(max(entries.shape))
    beside = spot[:widest] + [(spot[widest] + 1) % entries.shape[widest]] + spot[widest + 1:]
    return entries.at[tuple(spot)].set(low).at[tuple(beside)].set(largest)


def level_of(key, extent, shards, least, largest):
    gain, own = 1.0, jax.random.fold_in(key, 6)
    for position, parts in shards:
        steps = jnp.exp(jax.random.uniform(jax.random.fold_in(own, position), (parts,), jnp.float32, least / len(shards), largest / len(shards)))
        gain = gain * jnp.repeat(steps, extent[position] // parts).reshape([-1 if axis == position else 1 for axis in range(len(extent))])
    return gain


def normal_values(own_key, extent, spread, reach, cuts=(), held_as=jnp.bfloat16):
    entries = spread * jax.random.normal(own_key, extent, jnp.float32)
    if cuts:
        entries = entries * level_of(own_key, extent, cuts, -0.22, 0.18)
    return jnp.clip(entries, -reach, reach).astype(held_as)


def setup_inputs(seed: int = 0) -> dict:
    key_of = jax.random.split(jax.random.key(seed), 7)
    return {
        "initial": normal_values(key_of[0], (NODES, H), 1.0, 6.0, ((0, 64), (1, 4))),
        "history": normal_values(key_of[1], (LAYERS - 1, NODES, H), 1.0, 6.0, ((1, 64), (2, 4))),
        "adjacency": draw_adjacency(jax.random.fold_in(key_of[6], 71), 0),
        "tile_mask": draw_tile_mask(jax.random.fold_in(key_of[6], 71), 0),
        "send_lists": set_ends(jax.random.randint(key_of[4], (N_DOM, N_DOM, SLOT), 0, ROWS), jax.random.fold_in(key_of[4], 1), 0, ROWS - 1).astype(jnp.int32),
        "weights": normal_values(key_of[5], (LAYERS, H, H), H ** -0.5, 0.375, ((1, 4),)),
    }


def make_propagate(adj_rows, mask_rows):
    expand = jnp.repeat(jnp.repeat(mask_rows, TILE, axis=0), TILE, axis=1).astype(jnp.float32)
    masked = adj_rows.astype(jnp.float32) * expand
    return (masked / (1.0 + jnp.sum(masked, axis=1, keepdims=True))).astype(jnp.bfloat16)


def reference(initial, history, adjacency, tile_mask, send_lists, weights):
    adj_parts = adjacency.reshape(N_DOM, ROWS, ROWS + HALO)
    mask_parts = tile_mask.reshape(N_DOM, ROWS // TILE, (ROWS + HALO) // TILE)
    init_parts = initial.reshape(N_DOM, ROWS, H)
    current = init_parts
    for depth in range(LAYERS):
        source = init_parts if depth == 0 else history[depth - 1].reshape(N_DOM, ROWS, H)
        picked = source[jnp.arange(N_DOM)[:, None, None], send_lists]
        boundary = picked.transpose(1, 0, 2, 3).reshape(N_DOM, HALO, H)
        beta = jnp.log(0.5 / (depth + 1) + 1.0).astype(jnp.float32)
        weight = weights[depth]

        def one_part(items):
            adj_rows, mask_rows, rows_now, rows_halo, rows_init = items
            propagate = make_propagate(adj_rows, mask_rows)
            joined = jnp.concatenate([rows_now, rows_halo], axis=0)
            aggregate = jnp.dot(propagate, joined, preferred_element_type=jnp.float32)
            support = 0.9 * aggregate + 0.1 * rows_init.astype(jnp.float32)
            product = jnp.dot(support.astype(jnp.bfloat16), weight, preferred_element_type=jnp.float32)
            return jax.nn.relu((1.0 - beta) * support + beta * product).astype(jnp.bfloat16)

        current = lax.map(one_part, (adj_parts, mask_parts, current, boundary, init_parts))
    return current.reshape(NODES, H)
```

```python
import functools
import math

import jax
import jax.numpy as jnp
from jax import lax
from jax.experimental import pallas as pl
from jax.experimental.pallas import tpu as pltpu
from jax.sharding import PartitionSpec as P

TILE = 128
BF = jnp.bfloat16
F32 = jnp.float32
MIB = 2**20


def in_vmem(x):
    return pltpu.with_memory_space_constraint(x, pltpu.VMEM)


def nt_dot(a, b):
    return lax.dot_general(a, b, (((1,), (1,)), ((), ())), preferred_element_type=F32)


def pick_kernel(send_hbm, init_hbm, hist_hbm, weight_hbm, out_ref, pack_ref, send_ref, source_ref, weight_ref, sems):
    slots, peers = send_hbm.shape
    width, rows = init_hbm.shape
    layers = hist_hbm.shape[0] + 1
    copies = [pltpu.make_async_copy(init_hbm, source_ref.at[pl.ds(0, width), :], sems.at[0])]
    copies.append(pltpu.make_async_copy(weight_hbm, weight_ref, sems.at[1]))
    for k in range(layers - 1):
        place = source_ref.at[pl.ds((k + 1) * width, width), :]
        copies.append(pltpu.make_async_copy(hist_hbm.at[k], place, sems.at[k + 2]))
    lists_copy = pltpu.make_async_copy(send_hbm, send_ref, sems.at[layers + 1])
    lists_copy.start()
    for copy in copies:
        copy.start()
    lists_copy.wait()
    lists = send_ref[...].T
    spread = jnp.broadcast_to(lists[:, None, :], (peers, slots, slots)).reshape(peers * slots, slots)
    at = lax.broadcasted_iota(jnp.int32, spread.shape, 0) % slots
    lane = lax.broadcasted_iota(jnp.int32, spread.shape, 1)
    index = jnp.sum(jnp.where(at == lane, spread, 0), axis=1, keepdims=True)
    spare = out_ref.shape[1] - layers * width
    out_ref[:, layers * width :] = jnp.zeros((peers * slots, spare), BF)
    cols = weight_ref.shape[2]
    pieces = weight_ref.shape[0] * width // 32
    pack_ref[width:, pieces * cols :] = jnp.zeros((32, rows - pieces * cols), BF)
    copies[1].wait()
    flat = weight_ref[...].reshape(-1, cols)
    for piece in range(pieces):
        pack_ref[width:, piece * cols : (piece + 1) * cols] = flat[piece * 32 : (piece + 1) * 32]
    copies[0].wait()
    pack_ref[:width, :] = source_ref[:width, :]
    for copy in copies[2:]:
        copy.wait()
    step = 128
    for begin in range(0, peers * slots, step):
        node = lax.broadcasted_iota(jnp.int32, (step, rows), 1)
        chosen = jnp.where(node == index[begin : begin + step], 1.0, 0.0).astype(BF)
        out_ref[begin : begin + step, : layers * width] = nt_dot(chosen, source_ref[...]).astype(BF)


def turn_kernel(place_ref, p0, p1, p2, p3, init_ref, weight_ref):
    full = init_ref.shape[1]
    packs = (p0, p1, p2, p3)
    for k, pack in enumerate(packs):
        init_ref[:, k * 64 : (k + 1) * 64] = pack[:64, :].T
    turned = lax.broadcasted_iota(jnp.int32, (full, full), 1) + 64 * place_ref[0]
    turned = jnp.where(turned >= full, turned - full, turned)
    turn = jnp.where(lax.broadcasted_iota(jnp.int32, (full, full), 0) == turned, 1.0, 0.0).astype(BF)
    for k, pack in enumerate(packs):
        flat = jnp.concatenate([pack[64:, j * full : (j + 1) * full] for j in range(6)], axis=0)
        flat = jnp.dot(flat, turn, preferred_element_type=F32).astype(BF)
        for depth in range(3):
            weight_ref[depth, k * 64 : (k + 1) * 64, :] = flat[depth * 64 : (depth + 1) * 64]


def compact_kernel(got_ref, _, out_ref):
    halo = got_ref.shape[0]
    half = halo // 2
    out_ref[:halo, :] = got_ref[:, :128]
    out_ref[halo:, :64] = got_ref[:half, 128:192]
    out_ref[halo:, 64:] = got_ref[half:, 128:192]


def own_kernel(mask_ref, adj_hbm, init_hbm, _, masked_ref, scale_ref, sums_ref, rest_ref, init_ref, sems):
    rows, cols = masked_ref.shape
    chunk = rows // (sems.shape[0] - 1)
    first = pltpu.make_async_copy(init_hbm, init_ref, sems.at[rows // chunk])
    first.start()

    def copy(i):
        part = pl.ds(i * chunk, chunk)
        return pltpu.make_async_copy(adj_hbm.at[part, :], masked_ref.at[part, :], sems.at[i])

    for i in range(rows // chunk):
        copy(i).start()
    first.wait()
    rest_ref[...] = 0.1 * init_ref[...].astype(F32)
    for i in range(rows // TILE):
        if i * TILE % chunk == 0:
            copy(i * TILE // chunk).wait()
        part = pl.ds(i * TILE, TILE)
        total = jnp.zeros((TILE, TILE), F32)
        for t in range(cols // TILE):
            keep = mask_ref[i, t].astype(F32).astype(BF)
            tile = masked_ref[part, t * TILE : (t + 1) * TILE] * keep
            masked_ref[part, t * TILE : (t + 1) * TILE] = tile
            total += tile.astype(F32)
        scale = 0.9 / (1.0 + jnp.sum(total, axis=1, keepdims=True))
        scale_ref[part, :] = jnp.broadcast_to(scale, (TILE, scale_ref.shape[1]))
    block = 1024
    for begin in range(0, rows, block):
        part = pl.ds(begin, block)
        sums_ref[part, :] = jnp.dot(masked_ref[part, :rows], init_ref[...], preferred_element_type=F32)


def finish(depth, acc_ref, scale_ref, rest_ref, weight_ref, made_ref):
    step = 256
    beta = math.log(0.5 / (depth + 1) + 1.0)
    for begin in range(0, acc_ref.shape[0], step):
        part = pl.ds(begin, step)
        scale = jnp.concatenate([scale_ref[part, :]] * 2, axis=1)
        support = acc_ref[part, :] * scale + rest_ref[part, :]
        low = support.astype(BF)
        if depth == 2:
            product = jnp.dot(low, weight_ref[depth, :, :128], preferred_element_type=F32)
            made = jnp.maximum((1.0 - beta) * support[:, :128] + beta * product, 0.0)
            made_ref[:, part] = made.T[:64].astype(BF)
        else:
            product = jnp.dot(low, weight_ref[depth], preferred_element_type=F32)
            made = jnp.maximum((1.0 - beta) * support + beta * product, 0.0).astype(BF)
            made_ref[part, :] = made


def tail_kernel(masked_ref, scale_ref, sums_ref, rest_ref, weight_ref, b0, b1, b2, b3, out_ref, first, second, acc_ref):
    rows, cols = masked_ref.shape
    halo = cols - rows
    half = halo // 2
    packs = (b0, b1, b2, b3)
    block = 1024
    border = jnp.concatenate([pack[:halo, :64] for pack in packs], axis=1)
    first[rows:, :] = jnp.concatenate([pack[:halo, 64:] for pack in packs], axis=1)
    second[rows : rows + half, :] = jnp.concatenate([pack[halo:, :64] for pack in packs], axis=1)
    second[rows + half :, :] = jnp.concatenate([pack[halo:, 64:] for pack in packs], axis=1)
    for begin in range(0, rows, block):
        whole = pl.ds(begin, block)
        more = jnp.dot(masked_ref[whole, rows:], border, preferred_element_type=F32)
        acc_ref[whole, :] = sums_ref[whole, :] + more
    finish(0, acc_ref, scale_ref, rest_ref, weight_ref, first)
    for depth, joined, made_ref in ((1, first, second), (2, second, out_ref)):
        for begin in range(0, rows, block):
            whole = pl.ds(begin, block)
            acc_ref[whole, :] = jnp.dot(masked_ref[whole, :], joined[...], preferred_element_type=F32)
        finish(depth, acc_ref, scale_ref, rest_ref, weight_ref, made_ref)


def ring(x, shift):
    return lax.ppermute(x, "feat", [((i + shift) % 4, i) for i in range(4)])


def local(initial, history, adjacency, tile_mask, send_lists, weights):
    rows, width = initial.shape
    peers, slots = send_lists.shape[1:]
    halo = peers * slots
    cols = rows + halo
    full = weights.shape[2]
    vmem = pl.BlockSpec(memory_space=pltpu.VMEM)
    smem = pl.BlockSpec(memory_space=pltpu.SMEM)
    hbm = pl.BlockSpec(memory_space=pltpu.HBM)
    params = pltpu.CompilerParams
    place = lax.axis_index("feat").astype(jnp.int32).reshape(1)
    layers = weights.shape[0]

    def in_hbm(x):
        return pltpu.with_memory_space_constraint(x, pltpu.HBM)

    outgoing, pack = pl.pallas_call(
        pick_kernel,
        out_shape=[pltpu.VMEM((halo, full), BF), pltpu.VMEM((width + 32, rows), BF)],
        in_specs=[hbm] * 4,
        out_specs=[vmem] * 2,
        scratch_shapes=[
            pltpu.VMEM((slots, peers), jnp.int32),
            pltpu.VMEM((layers * width, rows), BF),
            pltpu.VMEM(weights.shape, BF),
            pltpu.SemaphoreType.DMA((layers + 2,)),
        ],
        compiler_params=params(vmem_limit_bytes=8 * MIB),
        name="pick",
    )(in_hbm(send_lists[0].T), in_hbm(initial.T), in_hbm(jnp.swapaxes(history, 1, 2)), in_hbm(weights))
    packs = [pack] + [ring(pack, shift) for shift in (1, 2, 3)]

    arrived = lax.all_to_all(outgoing.reshape(peers, slots, full), "dom", split_axis=0, concat_axis=0, tiled=True)
    whole_init, turned = pl.pallas_call(
        turn_kernel,
        out_shape=[jax.ShapeDtypeStruct((rows, full), BF), jax.ShapeDtypeStruct((layers, full, full), BF)],
        in_specs=[smem] + [vmem] * 4,
        out_specs=[vmem] * 2,
        compiler_params=params(vmem_limit_bytes=8 * MIB),
        cost_estimate=pl.CostEstimate(flops=8_000_000_000, bytes_accessed=4 * rows * full, transcendentals=0),
        name="turn",
    )(place, *[in_vmem(p) for p in packs])

    border = pl.pallas_call(
        compact_kernel,
        out_shape=pltpu.VMEM((halo + halo // 2, 128), BF),
        in_specs=[vmem, hbm],
        out_specs=vmem,
        compiler_params=params(vmem_limit_bytes=2 * MIB),
        name="compact",
    )(in_vmem(arrived.reshape(halo, full)), in_hbm(whole_init))
    borders = [border] + [ring(border, shift) for shift in (1, 2, 3)]

    masked, scale, sums, rest = pl.pallas_call(
        own_kernel,
        out_shape=[
            pltpu.VMEM((rows, cols), BF),
            pltpu.VMEM((rows, 128), F32),
            pltpu.VMEM((rows, full), F32),
            pltpu.VMEM((rows, full), F32),
        ],
        in_specs=[smem, hbm, hbm, vmem],
        out_specs=[vmem] * 4,
        scratch_shapes=[pltpu.VMEM((rows, full), BF), pltpu.SemaphoreType.DMA((9,))],
        compiler_params=params(vmem_limit_bytes=8 * MIB),
        cost_estimate=pl.CostEstimate(flops=4 * rows * rows * full, bytes_accessed=2 * rows * cols, transcendentals=0),
        name="own",
    )(tile_mask, in_hbm(adjacency), in_hbm(whole_init), in_vmem(border))

    out = pl.pallas_call(
        tail_kernel,
        out_shape=jax.ShapeDtypeStruct((width, rows), BF),
        in_specs=[vmem] * 9,
        out_specs=vmem,
        scratch_shapes=[pltpu.VMEM((cols, full), BF), pltpu.VMEM((cols, full), BF), pltpu.VMEM((rows, full), F32)],
        compiler_params=params(vmem_limit_bytes=12 * MIB),
        name="tail",
    )(*[in_vmem(x) for x in (masked, scale, sums, rest, turned, *borders)])
    return out.T


def solution(mesh):
    placed = (
        P("dom", "feat"),
        P(None, "dom", "feat"),
        P("dom", None),
        P("dom", None),
        P("dom", None, None),
        P(None, "feat", None),
    )
    return jax.shard_map(
        local, mesh=mesh, in_specs=placed, out_specs=P("dom", "feat"), check_vma=False
    )
```

```python
import functools
import math

import jax
import jax.numpy as jnp
from jax import lax
from jax.experimental import pallas as pl
from jax.experimental.pallas import tpu as pltpu
from jax.sharding import PartitionSpec as P

TILE = 128
BF = jnp.bfloat16
F32 = jnp.float32
MIB = 2**20


def in_vmem(x):
    return pltpu.with_memory_space_constraint(x, pltpu.VMEM)


def nt_dot(a, b):
    return lax.dot_general(a, b, (((1,), (1,)), ((), ())), preferred_element_type=F32)


def pick_kernel(send_hbm, init_hbm, hist_hbm, weight_hbm, out_ref, pack_a, pack_b, send_ref, chosen_ref, source_ref, weight_ref, sems):
    slots, peers = send_hbm.shape
    width, rows = init_hbm.shape
    layers = hist_hbm.shape[0] + 1
    copies = [pltpu.make_async_copy(init_hbm, source_ref.at[pl.ds(0, width), :], sems.at[0])]
    copies.append(pltpu.make_async_copy(weight_hbm, weight_ref, sems.at[1]))
    for k in range(layers - 1):
        place = source_ref.at[pl.ds((k + 1) * width, width), :]
        copies.append(pltpu.make_async_copy(hist_hbm.at[k], place, sems.at[k + 2]))
    lists_copy = pltpu.make_async_copy(send_hbm, send_ref, sems.at[layers + 1])
    lists_copy.start()
    for copy in copies:
        copy.start()
    lists_copy.wait()
    lists = send_ref[...].T
    spread = jnp.broadcast_to(lists[:, None, :], (peers, slots, slots)).reshape(peers * slots, slots)
    at = lax.broadcasted_iota(jnp.int32, spread.shape, 0) % slots
    lane = lax.broadcasted_iota(jnp.int32, spread.shape, 1)
    index = jnp.sum(jnp.where(at == lane, spread, 0), axis=1, keepdims=True)
    step = 64
    for begin in range(0, peers * slots, step):
        node = lax.broadcasted_iota(jnp.int32, (step, rows), 1)
        chosen_ref[begin : begin + step, :] = jnp.where(node == index[begin : begin + step], 1.0, 0.0).astype(BF)
    spare = out_ref.shape[1] - layers * width
    out_ref[:, layers * width :] = jnp.zeros((peers * slots, spare), BF)
    full = weight_ref.shape[2]
    parts = rows // full
    copies[1].wait()
    flat = weight_ref[...].reshape(-1, full)
    half = flat.shape[0] // 2
    for n, pack_ref in enumerate((pack_a, pack_b)):
        pack_ref[parts // 2 * width :, :] = flat[n * half : (n + 1) * half]
    copies[0].wait()
    for n, pack_ref in enumerate((pack_a, pack_b)):
        for j in range(parts // 2):
            begin = (n * parts // 2 + j) * full
            pack_ref[j * width : (j + 1) * width, :] = source_ref[:width, begin : begin + full]
    for copy in copies[2:]:
        copy.wait()
    out_ref[:, : layers * width] = nt_dot(chosen_ref[...], source_ref[...]).astype(BF)


def split_kernel(core_ref, got_ref, mine_ref, other_ref):
    chips = got_ref.shape[0]
    full = got_ref.shape[2]
    low, high = got_ref[:, :8, :], got_ref[:, 8:, :]
    first = core_ref[0] == 0
    mine_ref[...] = jnp.where(first, low, high).reshape(chips * 8, full)
    other_ref[...] = jnp.where(first, high, low).reshape(chips * 8, full)


def merge_kernel(core_ref, mine_ref, other_ref, out_ref):
    count, full = mine_ref.shape
    chips = count // 8
    halo = 2 * count
    first = core_ref[0] == 0
    mine = mine_ref[...].reshape(chips, 8, full)
    other = other_ref[...].reshape(chips, 8, full)
    low, high = jnp.where(first, mine, other), jnp.where(first, other, mine)
    got = jnp.concatenate([low, high], axis=1).reshape(halo, full)
    out_ref[:halo, :] = got[:, :128]
    out_ref[halo:, :64] = got[:count, 128:192]
    out_ref[halo:, 64:] = got[count:, 128:192]


def prep_kernel(mask_hbm, adj_hbm, _, __, ___, _a, _b, masked_ref, scale_ref, mask_ref, sems):
    rows, cols = masked_ref.shape
    chunk = rows // (sems.shape[0] - 1)
    mask_copy = pltpu.make_async_copy(mask_hbm, mask_ref, sems.at[rows // chunk])
    mask_copy.start()

    def copy(i):
        part = pl.ds(i * chunk, chunk)
        return pltpu.make_async_copy(adj_hbm.at[part, :], masked_ref.at[part, :], sems.at[i])

    for i in range(rows // chunk):
        copy(i).start()
    mask_copy.wait()
    for i in range(rows // TILE):
        if i * TILE % chunk == 0:
            copy(i * TILE // chunk).wait()
        part = pl.ds(i * TILE, TILE)
        total = jnp.zeros((TILE, TILE), F32)
        for t in range(cols // TILE):
            keep = mask_ref[i, t].astype(F32).astype(BF)
            tile = masked_ref[part, t * TILE : (t + 1) * TILE] * keep
            masked_ref[part, t * TILE : (t + 1) * TILE] = tile
            total += tile.astype(F32)
        scale = 0.9 / (1.0 + jnp.sum(total, axis=1, keepdims=True))
        scale_ref[part, :] = jnp.broadcast_to(scale, (TILE, scale_ref.shape[1]))


def own_kernel(place_ref, masked_ref, a0, a1, a2, a3, b0, b1, b2, b3, sums_ref, rest_ref, weight_ref, init_ref):
    rows = masked_ref.shape[0]
    full = init_ref.shape[1]
    width = full // 4
    parts = rows // full
    packs = ((a0, a1, a2, a3), (b0, b1, b2, b3))
    turned = lax.broadcasted_iota(jnp.int32, (full, full), 1) + width * place_ref[0]
    turned = jnp.where(turned >= full, turned - full, turned)
    turn = jnp.where(lax.broadcasted_iota(jnp.int32, (full, full), 0) == turned, 1.0, 0.0).astype(BF)
    for n, group in enumerate(packs):
        for j in range(parts // 2):
            piece = jnp.concatenate([pack[j * width : (j + 1) * width, :] for pack in group], axis=0)
            begin = (n * parts // 2 + j) * full
            init_ref[begin : begin + full, :] = piece.T
    begin = parts // 2 * width
    layers = weight_ref.shape[0]
    for k in range(4):
        flat = jnp.concatenate([group[k][begin:, :] for group in packs], axis=0)
        flat = jnp.dot(flat, turn, preferred_element_type=F32).astype(BF)
        for depth in range(layers):
            weight_ref[depth, k * width : (k + 1) * width, :] = flat[depth * width : (depth + 1) * width]
    block = 1024
    for begin in range(0, rows, block):
        part = pl.ds(begin, block)
        sums_ref[part, :] = jnp.dot(masked_ref[part, :rows], init_ref[...], preferred_element_type=F32)
    rest_ref[...] = 0.1 * init_ref[...].astype(F32)


def finish(depth, acc_ref, scale_ref, rest_ref, weight_ref, made_ref):
    step = 256
    beta = math.log(0.5 / (depth + 1) + 1.0)
    for begin in range(0, acc_ref.shape[0], step):
        part = pl.ds(begin, step)
        scale = jnp.concatenate([scale_ref[part, :]] * 2, axis=1)
        support = acc_ref[part, :] * scale + rest_ref[part, :]
        low = support.astype(BF)
        if depth == 2:
            product = jnp.dot(low, weight_ref[depth, :, :128], preferred_element_type=F32)
            made = jnp.maximum((1.0 - beta) * support[:, :128] + beta * product, 0.0)
            made_ref[:, part] = made.T[:64].astype(BF)
        else:
            product = jnp.dot(low, weight_ref[depth], preferred_element_type=F32)
            made = jnp.maximum((1.0 - beta) * support + beta * product, 0.0).astype(BF)
            made_ref[part, :] = made


def tail_kernel(masked_ref, scale_ref, sums_ref, rest_ref, weight_ref, b0, b1, b2, b3, out_ref, first, second, acc_ref):
    rows, cols = masked_ref.shape
    halo = cols - rows
    half = halo // 2
    packs = (b0, b1, b2, b3)
    block = 1024
    border = jnp.concatenate([pack[:halo, :64] for pack in packs], axis=1)
    first[rows:, :] = jnp.concatenate([pack[:halo, 64:] for pack in packs], axis=1)
    second[rows : rows + half, :] = jnp.concatenate([pack[halo:, :64] for pack in packs], axis=1)
    second[rows + half :, :] = jnp.concatenate([pack[halo:, 64:] for pack in packs], axis=1)
    for begin in range(0, rows, block):
        whole = pl.ds(begin, block)
        more = jnp.dot(masked_ref[whole, rows:], border, preferred_element_type=F32)
        acc_ref[whole, :] = sums_ref[whole, :] + more
    finish(0, acc_ref, scale_ref, rest_ref, weight_ref, first)
    for depth, joined, made_ref in ((1, first, second), (2, second, out_ref)):
        for begin in range(0, rows, block):
            whole = pl.ds(begin, block)
            acc_ref[whole, :] = jnp.dot(masked_ref[whole, :], joined[...], preferred_element_type=F32)
        finish(depth, acc_ref, scale_ref, rest_ref, weight_ref, made_ref)


def ring(x, shift):
    return lax.ppermute(x, "feat", [((i + shift) % 4, i) for i in range(4)])


def local(initial, history, adjacency, tile_mask, send_lists, weights):
    rows, width = initial.shape
    peers, slots = send_lists.shape[1:]
    halo = peers * slots
    cols = rows + halo
    full = weights.shape[2]
    vmem = pl.BlockSpec(memory_space=pltpu.VMEM)
    smem = pl.BlockSpec(memory_space=pltpu.SMEM)
    hbm = pl.BlockSpec(memory_space=pltpu.HBM)
    params = pltpu.CompilerParams
    place = lax.axis_index("feat").astype(jnp.int32).reshape(1)
    layers = weights.shape[0]

    def in_hbm(x):
        return pltpu.with_memory_space_constraint(x, pltpu.HBM)

    outgoing, pack_a, pack_b = pl.pallas_call(
        pick_kernel,
        out_shape=[pltpu.VMEM((halo, full), BF)] + [pltpu.VMEM(((rows // full + layers) * width // 2, full), BF)] * 2,
        in_specs=[hbm] * 4,
        out_specs=[vmem] * 3,
        scratch_shapes=[
            pltpu.VMEM((slots, peers), jnp.int32),
            pltpu.VMEM((halo, rows), BF),
            pltpu.VMEM((layers * width, rows), BF),
            pltpu.VMEM(weights.shape, BF),
            pltpu.SemaphoreType.DMA((layers + 2,)),
        ],
        compiler_params=params(vmem_limit_bytes=8 * MIB),
        name="pick",
    )(in_hbm(send_lists[0].T), in_hbm(initial.T), in_hbm(jnp.swapaxes(history, 1, 2)), in_hbm(weights))
    a1, a3 = ring(pack_a, 1), ring(pack_a, 3)
    b1, b3 = ring(pack_b, 1), ring(pack_b, 3)
    packs = [pack_a, a1, ring(a1, 1), a3, pack_b, b1, ring(b3, 3), b3]

    cores = 2
    chips = peers // cores
    core = lax.rem(lax.axis_index("dom"), cores).astype(jnp.int32).reshape(1)
    groups = [[chip * cores + c for chip in range(chips)] for c in range(cores)]
    arrived = lax.all_to_all(
        outgoing.reshape(chips, cores * slots, full), "dom", split_axis=0, concat_axis=0, tiled=True, axis_index_groups=groups
    )
    mine, other = pl.pallas_call(
        split_kernel,
        out_shape=[pltpu.VMEM((halo // 2, full), BF)] * 2,
        in_specs=[smem, vmem],
        out_specs=[vmem] * 2,
        compiler_params=params(vmem_limit_bytes=4 * MIB),
        name="split",
    )(core, in_vmem(arrived))
    swap = [(i, i ^ 1) for i in range(peers)]
    border = pl.pallas_call(
        merge_kernel,
        out_shape=pltpu.VMEM((halo + halo // 2, 128), BF),
        in_specs=[smem, vmem, vmem],
        out_specs=vmem,
        compiler_params=params(vmem_limit_bytes=4 * MIB),
        name="merge",
    )(core, in_vmem(mine), in_vmem(lax.ppermute(other, "dom", swap)))
    borders = [border] + [ring(border, shift) for shift in (1, 2, 3)]

    masked, scale = pl.pallas_call(
        prep_kernel,
        out_shape=[pltpu.VMEM((rows, cols), BF), pltpu.VMEM((rows, 128), F32)],
        in_specs=[hbm, hbm] + [vmem] * 5,
        out_specs=[vmem] * 2,
        scratch_shapes=[pltpu.SMEM(tile_mask.shape, jnp.int32), pltpu.SemaphoreType.DMA((9,))],
        compiler_params=params(vmem_limit_bytes=4 * MIB),
        cost_estimate=pl.CostEstimate(flops=4_300_000_000, bytes_accessed=1000, transcendentals=0),
        name="prep",
    )(in_hbm(tile_mask), in_hbm(adjacency), in_vmem(border), *[in_vmem(packs[k]) for k in (2, 6, 3, 5)])

    sums, rest, turned = pl.pallas_call(
        own_kernel,
        out_shape=[
            pltpu.VMEM((rows, full), F32),
            pltpu.VMEM((rows, full), F32),
            pltpu.VMEM((layers, full, full), BF),
        ],
        in_specs=[smem] + [vmem] * 9,
        out_specs=[vmem] * 3,
        scratch_shapes=[pltpu.VMEM((rows, full), BF)],
        compiler_params=params(vmem_limit_bytes=8 * MIB),
        cost_estimate=pl.CostEstimate(flops=1000, bytes_accessed=1000, transcendentals=0),
        name="own",
    )(place, in_vmem(masked), *[in_vmem(p) for p in packs])

    out = pl.pallas_call(
        tail_kernel,
        out_shape=jax.ShapeDtypeStruct((width, rows), BF),
        in_specs=[vmem] * 9,
        out_specs=vmem,
        scratch_shapes=[pltpu.VMEM((cols, full), BF), pltpu.VMEM((cols, full), BF), pltpu.VMEM((rows, full), F32)],
        compiler_params=params(vmem_limit_bytes=12 * MIB),
        name="tail",
    )(*[in_vmem(x) for x in (masked, scale, sums, rest, turned, *borders)])
    return out.T


def solution(mesh):
    placed = (
        P("dom", "feat"),
        P(None, "dom", "feat"),
        P("dom", None),
        P("dom", None),
        P("dom", None, None),
        P(None, "feat", None),
    )
    return jax.shard_map(
        local, mesh=mesh, in_specs=placed, out_specs=P("dom", "feat"), check_vma=False
    )
```

```python
import functools
import math

import jax
import jax.numpy as jnp
from jax import lax
from jax.experimental import pallas as pl
from jax.experimental.pallas import tpu as pltpu
from jax.sharding import PartitionSpec as P

TILE = 128
BF = jnp.bfloat16
F32 = jnp.float32
MIB = 2**20


def in_vmem(x):
    return pltpu.with_memory_space_constraint(x, pltpu.VMEM)


def nt_dot(a, b):
    return lax.dot_general(a, b, (((1,), (1,)), ((), ())), preferred_element_type=F32)


def pick_kernel(send_hbm, init_hbm, hist_hbm, weight_hbm, out_ref, pack_a, pack_b, send_ref, chosen_ref, source_ref, weight_ref, sems):
    slots, peers = send_hbm.shape
    width, rows = init_hbm.shape
    layers = hist_hbm.shape[0] + 1
    copies = [pltpu.make_async_copy(init_hbm, source_ref.at[pl.ds(0, width), :], sems.at[0])]
    copies.append(pltpu.make_async_copy(weight_hbm, weight_ref, sems.at[1]))
    for k in range(layers - 1):
        place = source_ref.at[pl.ds((k + 1) * width, width), :]
        copies.append(pltpu.make_async_copy(hist_hbm.at[k], place, sems.at[k + 2]))
    lists_copy = pltpu.make_async_copy(send_hbm, send_ref, sems.at[layers + 1])
    lists_copy.start()
    for copy in copies:
        copy.start()
    lists_copy.wait()
    lists = send_ref[...].T
    spread = jnp.broadcast_to(lists[:, None, :], (peers, slots, slots)).reshape(peers * slots, slots)
    at = lax.broadcasted_iota(jnp.int32, spread.shape, 0) % slots
    lane = lax.broadcasted_iota(jnp.int32, spread.shape, 1)
    index = jnp.sum(jnp.where(at == lane, spread, 0), axis=1, keepdims=True)
    step = 64
    for begin in range(0, peers * slots, step):
        node = lax.broadcasted_iota(jnp.int32, (step, rows), 1)
        chosen_ref[begin : begin + step, :] = jnp.where(node == index[begin : begin + step], 1.0, 0.0).astype(BF)
    spare = out_ref.shape[1] - layers * width
    out_ref[:, layers * width :] = jnp.zeros((peers * slots, spare), BF)
    full = weight_ref.shape[2]
    parts = rows // full
    copies[1].wait()
    flat = weight_ref[...].reshape(-1, full)
    half = flat.shape[0] // 2
    for n, pack_ref in enumerate((pack_a, pack_b)):
        pack_ref[parts // 2 * width :, :] = flat[n * half : (n + 1) * half]
    copies[0].wait()
    for n, pack_ref in enumerate((pack_a, pack_b)):
        for j in range(parts // 2):
            begin = (n * parts // 2 + j) * full
            pack_ref[j * width : (j + 1) * width, :] = source_ref[:width, begin : begin + full]
    for copy in copies[2:]:
        copy.wait()
    out_ref[:, : layers * width] = nt_dot(chosen_ref[...], source_ref[...]).astype(BF)


def compact_kernel(got_ref, near_ref, far_ref, whole_ref):
    halo = got_ref.shape[0]
    half = halo // 2
    near_ref[:, :64] = got_ref[:half, :64]
    near_ref[:, 64:] = got_ref[half:, :64]
    far = got_ref[:, 64:192]
    far_ref[...] = far
    whole_ref[:half, :64] = got_ref[:half, :64]
    whole_ref[:half, 64:] = got_ref[half:, :64]
    whole_ref[half:, :] = far


def prep_kernel(mask_ref, adj_ref, _, __, ___, _a, _b, masked_ref, scale_ref):
    rows, cols = masked_ref.shape
    for i in range(rows // TILE):
        part = pl.ds(i * TILE, TILE)
        total = jnp.zeros((TILE, TILE), F32)
        for t in range(cols // TILE):
            keep = mask_ref[i, t].astype(F32).astype(BF)
            tile = adj_ref[part, t * TILE : (t + 1) * TILE] * keep
            masked_ref[part, t * TILE : (t + 1) * TILE] = tile
            total += tile.astype(F32)
        scale = 0.9 / (1.0 + jnp.sum(total, axis=1, keepdims=True))
        scale_ref[part, :] = jnp.broadcast_to(scale, (TILE, scale_ref.shape[1]))


def own_kernel(place_ref, masked_ref, a0, a1, a2, a3, b0, b1, b2, b3, sums_ref, rest_ref, weight_ref, init_ref):
    rows = masked_ref.shape[0]
    full = init_ref.shape[1]
    width = full // 4
    parts = rows // full
    packs = ((a0, a1, a2, a3), (b0, b1, b2, b3))
    turned = lax.broadcasted_iota(jnp.int32, (full, full), 1) + width * place_ref[0]
    turned = jnp.where(turned >= full, turned - full, turned)
    turn = jnp.where(lax.broadcasted_iota(jnp.int32, (full, full), 0) == turned, 1.0, 0.0).astype(BF)
    for n, group in enumerate(packs):
        for j in range(parts // 2):
            piece = jnp.concatenate([pack[j * width : (j + 1) * width, :] for pack in group], axis=0)
            begin = (n * parts // 2 + j) * full
            init_ref[begin : begin + full, :] = piece.T
    begin = parts // 2 * width
    layers = weight_ref.shape[0]
    for k in range(4):
        flat = jnp.concatenate([group[k][begin:, :] for group in packs], axis=0)
        flat = jnp.dot(flat, turn, preferred_element_type=F32).astype(BF)
        for depth in range(layers):
            weight_ref[depth, k * width : (k + 1) * width, :] = flat[depth * width : (depth + 1) * width]
    block = 1024
    for begin in range(0, rows, block):
        part = pl.ds(begin, block)
        sums_ref[part, :] = jnp.dot(masked_ref[part, :rows], init_ref[...], preferred_element_type=F32)
    rest_ref[...] = 0.1 * init_ref[...].astype(F32)


def finish(depth, acc_ref, scale_ref, rest_ref, weight_ref, made_ref):
    step = 256
    beta = math.log(0.5 / (depth + 1) + 1.0)
    for begin in range(0, acc_ref.shape[0], step):
        part = pl.ds(begin, step)
        scale = jnp.concatenate([scale_ref[part, :]] * 2, axis=1)
        support = acc_ref[part, :] * scale + rest_ref[part, :]
        low = support.astype(BF)
        if depth == 2:
            product = jnp.dot(low, weight_ref[depth, :, :128], preferred_element_type=F32)
            made = jnp.maximum((1.0 - beta) * support[:, :128] + beta * product, 0.0)
            made_ref[:, part] = made.T[:64].astype(BF)
        else:
            product = jnp.dot(low, weight_ref[depth], preferred_element_type=F32)
            made = jnp.maximum((1.0 - beta) * support + beta * product, 0.0).astype(BF)
            made_ref[part, :] = made


def early_kernel(masked_ref, scale_ref, sums_ref, rest_ref, weight_ref, b0, b1, b2, b3, next_ref, border, made, acc_ref):
    rows, cols = masked_ref.shape
    half = b2.shape[0]
    packs = [pack[:half, :] for pack in (b0, b1, b2, b3)]
    block = 1024
    border[:half, :] = jnp.concatenate([pack[:, :64] for pack in packs], axis=1)
    border[half:, :] = jnp.concatenate([pack[:, 64:] for pack in packs], axis=1)
    for begin in range(0, rows, block):
        whole = pl.ds(begin, block)
        more = jnp.dot(masked_ref[whole, rows:], border[...], preferred_element_type=F32)
        acc_ref[whole, :] = sums_ref[whole, :] + more
    finish(0, acc_ref, scale_ref, rest_ref, weight_ref, made)
    for begin in range(0, rows, block):
        whole = pl.ds(begin, block)
        next_ref[whole, :] = jnp.dot(masked_ref[whole, :rows], made[...], preferred_element_type=F32)


def late_kernel(masked_ref, scale_ref, sums_ref, rest_ref, weight_ref, b0, b1, b2, b3, out_ref, joined, acc_ref):
    rows, cols = masked_ref.shape
    half = (cols - rows) // 2
    packs = (b0[half:, :], b1[half:, :], b2[...], b3[half:, :])
    block = 1024
    border = jnp.concatenate([pack[:, :64] for pack in packs], axis=1)
    joined[rows:, :] = jnp.concatenate([pack[:, 64:] for pack in packs], axis=1)
    for begin in range(0, rows, block):
        whole = pl.ds(begin, block)
        more = jnp.dot(masked_ref[whole, rows:], border, preferred_element_type=F32)
        acc_ref[whole, :] = sums_ref[whole, :] + more
    finish(1, acc_ref, scale_ref, rest_ref, weight_ref, joined)
    for begin in range(0, rows, block):
        whole = pl.ds(begin, block)
        acc_ref[whole, :] = jnp.dot(masked_ref[whole, :], joined[...], preferred_element_type=F32)
    finish(2, acc_ref, scale_ref, rest_ref, weight_ref, out_ref)


def ring(x, shift):
    return lax.ppermute(x, "feat", [((i + shift) % 4, i) for i in range(4)])


def local(initial, history, adjacency, tile_mask, send_lists, weights):
    rows, width = initial.shape
    peers, slots = send_lists.shape[1:]
    halo = peers * slots
    cols = rows + halo
    full = weights.shape[2]
    vmem = pl.BlockSpec(memory_space=pltpu.VMEM)
    smem = pl.BlockSpec(memory_space=pltpu.SMEM)
    hbm = pl.BlockSpec(memory_space=pltpu.HBM)
    params = pltpu.CompilerParams
    place = lax.axis_index("feat").astype(jnp.int32).reshape(1)
    layers = weights.shape[0]

    def in_hbm(x):
        return pltpu.with_memory_space_constraint(x, pltpu.HBM)

    outgoing, pack_a, pack_b = pl.pallas_call(
        pick_kernel,
        out_shape=[pltpu.VMEM((halo, full), BF)] + [pltpu.VMEM(((rows // full + layers) * width // 2, full), BF)] * 2,
        in_specs=[hbm] * 4,
        out_specs=[vmem] * 3,
        scratch_shapes=[
            pltpu.VMEM((slots, peers), jnp.int32),
            pltpu.VMEM((halo, rows), BF),
            pltpu.VMEM((layers * width, rows), BF),
            pltpu.VMEM(weights.shape, BF),
            pltpu.SemaphoreType.DMA((layers + 2,)),
        ],
        compiler_params=params(vmem_limit_bytes=8 * MIB),
        name="pick",
    )(in_hbm(send_lists[0].T), in_hbm(initial.T), in_hbm(jnp.swapaxes(history, 1, 2)), in_hbm(weights))
    a1, a3 = ring(pack_a, 1), ring(pack_a, 3)
    b1, b3 = ring(pack_b, 1), ring(pack_b, 3)
    packs = [pack_a, a1, ring(a1, 1), a3, pack_b, b1, ring(b3, 3), b3]

    arrived = lax.all_to_all(outgoing.reshape(peers, slots, full), "dom", split_axis=0, concat_axis=0, tiled=True)
    near, far, whole = pl.pallas_call(
        compact_kernel,
        out_shape=[pltpu.VMEM((size, 128), BF) for size in (halo // 2, halo, halo + halo // 2)],
        in_specs=[vmem],
        out_specs=[vmem] * 3,
        compiler_params=params(vmem_limit_bytes=2 * MIB),
        cost_estimate=pl.CostEstimate(flops=15000000000, bytes_accessed=1000, transcendentals=0),
        name="compact",
    )(in_vmem(arrived.reshape(halo, full)))
    after_all, before_all = ring(whole, 1), ring(whole, 3)
    nears = [whole, after_all, ring(near, 2), before_all]
    fars = [whole, after_all, ring(far, 2), before_all]

    masked, scale = pl.pallas_call(
        prep_kernel,
        out_shape=[pltpu.VMEM((rows, cols), BF), pltpu.VMEM((rows, 128), F32)],
        in_specs=[smem] + [vmem] * 6,
        out_specs=[vmem] * 2,
        compiler_params=params(vmem_limit_bytes=14 * MIB),
        cost_estimate=pl.CostEstimate(flops=4300001000, bytes_accessed=1000, transcendentals=0),
        name="prep",
    )(tile_mask, adjacency, in_vmem(near), *[in_vmem(packs[k]) for k in (2, 6, 3, 5)])

    sums, rest, turned = pl.pallas_call(
        own_kernel,
        out_shape=[
            pltpu.VMEM((rows, full), F32),
            pltpu.VMEM((rows, full), F32),
            pltpu.VMEM((layers, full, full), BF),
        ],
        in_specs=[smem] + [vmem] * 9,
        out_specs=[vmem] * 3,
        scratch_shapes=[pltpu.VMEM((rows, full), BF)],
        compiler_params=params(vmem_limit_bytes=8 * MIB),
        cost_estimate=pl.CostEstimate(flops=2100001000, bytes_accessed=1000, transcendentals=0),
        name="own",
    )(place, in_vmem(masked), *[in_vmem(p) for p in packs])

    sums = pl.pallas_call(
        early_kernel,
        out_shape=pltpu.VMEM((rows, full), F32),
        in_specs=[vmem] * 9,
        out_specs=vmem,
        scratch_shapes=[pltpu.VMEM((halo, full), BF), pltpu.VMEM((rows, full), BF), pltpu.VMEM((rows, full), F32)],
        compiler_params=params(vmem_limit_bytes=10 * MIB),
        cost_estimate=pl.CostEstimate(flops=1000, bytes_accessed=1000, transcendentals=0),
        name="early",
    )(*[in_vmem(x) for x in (masked, scale, sums, rest, turned, *nears)])

    out = pl.pallas_call(
        late_kernel,
        out_shape=jax.ShapeDtypeStruct((width, rows), BF),
        in_specs=[vmem] * 9,
        out_specs=vmem,
        scratch_shapes=[pltpu.VMEM((cols, full), BF), pltpu.VMEM((rows, full), F32)],
        compiler_params=params(vmem_limit_bytes=10 * MIB),
        name="late",
    )(*[in_vmem(x) for x in (masked, scale, sums, rest, turned, *fars)])
    return out.T


def solution(mesh):
    placed = (
        P("dom", "feat"),
        P(None, "dom", "feat"),
        P("dom", None),
        P("dom", None),
        P("dom", None, None),
        P(None, "feat", None),
    )
    return jax.shard_map(
        local, mesh=mesh, in_specs=placed, out_specs=P("dom", "feat"), check_vma=False
    )
```

```python
import functools
import math

import jax
import jax.numpy as jnp
from jax import lax
from jax.experimental import pallas as pl
from jax.experimental.pallas import tpu as pltpu
from jax.sharding import PartitionSpec as P

TILE = 128
BF = jnp.bfloat16
F32 = jnp.float32
MIB = 2**20


def in_vmem(x):
    return pltpu.with_memory_space_constraint(x, pltpu.VMEM)


def nt_dot(a, b):
    return lax.dot_general(a, b, (((1,), (1,)), ((), ())), preferred_element_type=F32)


def pick_kernel(send_hbm, init_hbm, hist_hbm, weight_hbm, out_ref, pack_a, pack_b, send_ref, chosen_ref, source_ref, weight_ref, sems):
    slots, peers = send_hbm.shape
    width, rows = init_hbm.shape
    layers = hist_hbm.shape[0] + 1
    copies = [pltpu.make_async_copy(init_hbm, source_ref.at[pl.ds(0, width), :], sems.at[0])]
    copies.append(pltpu.make_async_copy(weight_hbm, weight_ref, sems.at[1]))
    for k in range(layers - 1):
        place = source_ref.at[pl.ds((k + 1) * width, width), :]
        copies.append(pltpu.make_async_copy(hist_hbm.at[k], place, sems.at[k + 2]))
    lists_copy = pltpu.make_async_copy(send_hbm, send_ref, sems.at[layers + 1])
    lists_copy.start()
    for copy in copies:
        copy.start()
    lists_copy.wait()
    lists = send_ref[...].T
    spread = jnp.broadcast_to(lists[:, None, :], (peers, slots, slots)).reshape(peers * slots, slots)
    at = lax.broadcasted_iota(jnp.int32, spread.shape, 0) % slots
    lane = lax.broadcasted_iota(jnp.int32, spread.shape, 1)
    index = jnp.sum(jnp.where(at == lane, spread, 0), axis=1, keepdims=True)
    step = 64
    for begin in range(0, peers * slots, step):
        node = lax.broadcasted_iota(jnp.int32, (step, rows), 1)
        chosen_ref[begin : begin + step, :] = jnp.where(node == index[begin : begin + step], 1.0, 0.0).astype(BF)
    spare = out_ref.shape[1] - layers * width
    out_ref[:, layers * width :] = jnp.zeros((peers * slots, spare), BF)
    full = weight_ref.shape[2]
    parts = rows // full
    copies[1].wait()
    flat = weight_ref[...].reshape(-1, full)
    half = flat.shape[0] // 2
    for n, pack_ref in enumerate((pack_a, pack_b)):
        pack_ref[parts // 2 * width :, :] = flat[n * half : (n + 1) * half]
    copies[0].wait()
    for n, pack_ref in enumerate((pack_a, pack_b)):
        for j in range(parts // 2):
            begin = (n * parts // 2 + j) * full
            pack_ref[j * width : (j + 1) * width, :] = source_ref[:width, begin : begin + full]
    for copy in copies[2:]:
        copy.wait()
    out_ref[:, : layers * width] = nt_dot(chosen_ref[...], source_ref[...]).astype(BF)


def compact_kernel(got_ref, near_ref, far_ref, whole_ref):
    halo = got_ref.shape[0]
    half = halo // 2
    near_ref[:, :64] = got_ref[:half, :64]
    near_ref[:, 64:] = got_ref[half:, :64]
    far = got_ref[:, 64:192]
    far_ref[...] = far
    whole_ref[:half, :64] = got_ref[:half, :64]
    whole_ref[:half, 64:] = got_ref[half:, :64]
    whole_ref[half:, :] = far


def prep_kernel(mask_ref, adj_ref, far_ref, _, __, ___, masked_ref, scale_ref, later_ref):
    later_ref[...] = far_ref[...]
    rows, cols = masked_ref.shape
    step = 16
    for i in range(rows // TILE):
        keep = [jnp.full((1, TILE), mask_ref[i, t].astype(F32), F32) for t in range(cols // TILE)]
        keep = jnp.concatenate(keep, axis=1).astype(BF)
        for begin in range(i * TILE, (i + 1) * TILE, step):
            part = pl.ds(begin, step)
            held = adj_ref[part, :] * keep
            masked_ref[part, :] = held
            wide = held.astype(F32)
            total = wide[:, :TILE]
            for t in range(1, cols // TILE):
                total = total + wide[:, t * TILE : (t + 1) * TILE]
            scale = 0.9 / (1.0 + jnp.sum(total, axis=1, keepdims=True))
            scale_ref[part, :] = jnp.broadcast_to(scale, (step, scale_ref.shape[1]))


def own_kernel(place_ref, masked_ref, a0, a1, a2, a3, b0, b1, b2, b3, sums_ref, rest_ref, weight_ref, init_ref):
    rows = masked_ref.shape[0]
    full = init_ref.shape[1]
    width = full // 4
    parts = rows // full
    packs = ((a0, a1, a2, a3), (b0, b1, b2, b3))
    turned = lax.broadcasted_iota(jnp.int32, (full, full), 1) + width * place_ref[0]
    turned = jnp.where(turned >= full, turned - full, turned)
    turn = jnp.where(lax.broadcasted_iota(jnp.int32, (full, full), 0) == turned, 1.0, 0.0).astype(BF)
    for n, group in enumerate(packs):
        for j in range(parts // 2):
            piece = jnp.concatenate([pack[j * width : (j + 1) * width, :] for pack in group], axis=0)
            begin = (n * parts // 2 + j) * full
            init_ref[begin : begin + full, :] = piece.T
    begin = parts // 2 * width
    layers = weight_ref.shape[0]
    for k in range(4):
        flat = jnp.concatenate([group[k][begin:, :] for group in packs], axis=0)
        flat = jnp.dot(flat, turn, preferred_element_type=F32).astype(BF)
        for depth in range(layers):
            weight_ref[depth, k * width : (k + 1) * width, :] = flat[depth * width : (depth + 1) * width]
    block = 1024
    for begin in range(0, rows, block):
        part = pl.ds(begin, block)
        sums_ref[part, :] = jnp.dot(masked_ref[part, :rows], init_ref[...], preferred_element_type=F32)
    rest_ref[...] = 0.1 * init_ref[...].astype(F32)


def finish(depth, acc_ref, scale_ref, rest_ref, weight_ref, made_ref):
    step = 256
    beta = math.log(0.5 / (depth + 1) + 1.0)
    for begin in range(0, acc_ref.shape[0], step):
        part = pl.ds(begin, step)
        scale = jnp.concatenate([scale_ref[part, :]] * 2, axis=1)
        support = acc_ref[part, :] * scale + rest_ref[part, :]
        low = support.astype(BF)
        if depth == 2:
            product = jnp.dot(low, weight_ref[depth, :, :128], preferred_element_type=F32)
            made = jnp.maximum((1.0 - beta) * support[:, :128] + beta * product, 0.0)
            made_ref[:, part] = made.T[:64].astype(BF)
        else:
            product = jnp.dot(low, weight_ref[depth], preferred_element_type=F32)
            made = jnp.maximum((1.0 - beta) * support + beta * product, 0.0).astype(BF)
            made_ref[part, :] = made


def early_kernel(masked_ref, scale_ref, sums_ref, rest_ref, weight_ref, b0, b1, b2, b3, next_ref, border, made, acc_ref):
    rows, cols = masked_ref.shape
    half = b2.shape[0]
    packs = [pack[:half, :] for pack in (b0, b1, b2, b3)]
    block = 1024
    border[:half, :] = jnp.concatenate([pack[:, :64] for pack in packs], axis=1)
    border[half:, :] = jnp.concatenate([pack[:, 64:] for pack in packs], axis=1)
    for begin in range(0, rows, block):
        whole = pl.ds(begin, block)
        more = jnp.dot(masked_ref[whole, rows:], border[...], preferred_element_type=F32)
        acc_ref[whole, :] = sums_ref[whole, :] + more
    finish(0, acc_ref, scale_ref, rest_ref, weight_ref, made)
    for begin in range(0, rows, block):
        whole = pl.ds(begin, block)
        next_ref[whole, :] = jnp.dot(masked_ref[whole, :rows], made[...], preferred_element_type=F32)


def late_kernel(masked_ref, scale_ref, sums_ref, rest_ref, weight_ref, b0, b1, b2, b3, out_ref, joined, acc_ref):
    rows, cols = masked_ref.shape
    half = (cols - rows) // 2
    packs = (b0[half:, :], b1[half:, :], b2[...], b3[half:, :])
    block = 1024
    border = jnp.concatenate([pack[:, :64] for pack in packs], axis=1)
    joined[rows:, :] = jnp.concatenate([pack[:, 64:] for pack in packs], axis=1)
    for begin in range(0, rows, block):
        whole = pl.ds(begin, block)
        more = jnp.dot(masked_ref[whole, rows:], border, preferred_element_type=F32)
        acc_ref[whole, :] = sums_ref[whole, :] + more
    finish(1, acc_ref, scale_ref, rest_ref, weight_ref, joined)
    for begin in range(0, rows, block):
        whole = pl.ds(begin, block)
        acc_ref[whole, :] = jnp.dot(masked_ref[whole, :], joined[...], preferred_element_type=F32)
    finish(2, acc_ref, scale_ref, rest_ref, weight_ref, out_ref)


def ring(x, shift):
    return lax.ppermute(x, "feat", [((i + shift) % 4, i) for i in range(4)])


def local(initial, history, adjacency, tile_mask, send_lists, weights):
    rows, width = initial.shape
    peers, slots = send_lists.shape[1:]
    halo = peers * slots
    cols = rows + halo
    full = weights.shape[2]
    vmem = pl.BlockSpec(memory_space=pltpu.VMEM)
    smem = pl.BlockSpec(memory_space=pltpu.SMEM)
    hbm = pl.BlockSpec(memory_space=pltpu.HBM)
    params = pltpu.CompilerParams
    place = lax.axis_index("feat").astype(jnp.int32).reshape(1)
    layers = weights.shape[0]

    def in_hbm(x):
        return pltpu.with_memory_space_constraint(x, pltpu.HBM)

    outgoing, pack_a, pack_b = pl.pallas_call(
        pick_kernel,
        out_shape=[pltpu.VMEM((halo, full), BF)] + [pltpu.VMEM(((rows // full + layers) * width // 2, full), BF)] * 2,
        in_specs=[hbm] * 4,
        out_specs=[vmem] * 3,
        scratch_shapes=[
            pltpu.VMEM((slots, peers), jnp.int32),
            pltpu.VMEM((halo, rows), BF),
            pltpu.VMEM((layers * width, rows), BF),
            pltpu.VMEM(weights.shape, BF),
            pltpu.SemaphoreType.DMA((layers + 2,)),
        ],
        compiler_params=params(vmem_limit_bytes=8 * MIB),
        name="pick",
    )(in_hbm(send_lists[0].T), in_hbm(initial.T), in_hbm(jnp.swapaxes(history, 1, 2)), in_hbm(weights))
    a1, a3 = ring(pack_a, 1), ring(pack_a, 3)
    b1, b3 = ring(pack_b, 1), ring(pack_b, 3)
    packs = [pack_a, a1, ring(a1, 1), a3, pack_b, b1, ring(b3, 3), b3]

    arrived = lax.all_to_all(outgoing.reshape(peers, slots, full), "dom", split_axis=0, concat_axis=0, tiled=True)
    near, far, whole = pl.pallas_call(
        compact_kernel,
        out_shape=[pltpu.VMEM((size, 128), BF) for size in (halo // 2, halo, halo + halo // 2)],
        in_specs=[vmem],
        out_specs=[vmem] * 3,
        compiler_params=params(vmem_limit_bytes=2 * MIB),
        cost_estimate=pl.CostEstimate(flops=15000000000, bytes_accessed=1000, transcendentals=0),
        name="compact",
    )(in_vmem(arrived.reshape(halo, full)))
    after_all, before_all = ring(whole, 1), ring(whole, 3)
    nears = [whole, after_all, ring(near, 2), before_all]

    masked, scale, later = pl.pallas_call(
        prep_kernel,
        out_shape=[pltpu.VMEM((rows, cols), BF), pltpu.VMEM((rows, 128), F32), pltpu.VMEM((halo, 128), BF)],
        in_specs=[smem] + [vmem] * 5,
        out_specs=[vmem] * 3,
        compiler_params=params(vmem_limit_bytes=14 * MIB),
        cost_estimate=pl.CostEstimate(flops=4300001000, bytes_accessed=1000, transcendentals=0),
        name="prep",
    )(tile_mask, adjacency, in_vmem(far), *[in_vmem(packs[k]) for k in (2, 3, 5)])

    fars = [whole, after_all, ring(later, 2), before_all]
    sums, rest, turned = pl.pallas_call(
        own_kernel,
        out_shape=[
            pltpu.VMEM((rows, full), F32),
            pltpu.VMEM((rows, full), F32),
            pltpu.VMEM((layers, full, full), BF),
        ],
        in_specs=[smem] + [vmem] * 9,
        out_specs=[vmem] * 3,
        scratch_shapes=[pltpu.VMEM((rows, full), BF)],
        compiler_params=params(vmem_limit_bytes=8 * MIB),
        cost_estimate=pl.CostEstimate(flops=2100001000, bytes_accessed=1000, transcendentals=0),
        name="own",
    )(place, in_vmem(masked), *[in_vmem(p) for p in packs])

    sums = pl.pallas_call(
        early_kernel,
        out_shape=pltpu.VMEM((rows, full), F32),
        in_specs=[vmem] * 9,
        out_specs=vmem,
        scratch_shapes=[pltpu.VMEM((halo, full), BF), pltpu.VMEM((rows, full), BF), pltpu.VMEM((rows, full), F32)],
        compiler_params=params(vmem_limit_bytes=10 * MIB),
        cost_estimate=pl.CostEstimate(flops=1000, bytes_accessed=1000, transcendentals=0),
        name="early",
    )(*[in_vmem(x) for x in (masked, scale, sums, rest, turned, *nears)])

    out = pl.pallas_call(
        late_kernel,
        out_shape=jax.ShapeDtypeStruct((width, rows), BF),
        in_specs=[vmem] * 9,
        out_specs=vmem,
        scratch_shapes=[pltpu.VMEM((cols, full), BF), pltpu.VMEM((rows, full), F32)],
        compiler_params=params(vmem_limit_bytes=10 * MIB),
        name="late",
    )(*[in_vmem(x) for x in (masked, scale, sums, rest, turned, *fars)])
    return out.T


def solution(mesh):
    placed = (
        P("dom", "feat"),
        P(None, "dom", "feat"),
        P("dom", None),
        P("dom", None),
        P("dom", None, None),
        P(None, "feat", None),
    )
    return jax.shard_map(
        local, mesh=mesh, in_specs=placed, out_specs=P("dom", "feat"), check_vma=False
    )
```

```python
import functools
import math

import jax
import jax.numpy as jnp
from jax import lax
from jax.experimental import pallas as pl
from jax.experimental.pallas import tpu as pltpu
from jax.sharding import PartitionSpec as P

TILE = 128
BF = jnp.bfloat16
F32 = jnp.float32
MIB = 2**20


def in_vmem(x):
    return pltpu.with_memory_space_constraint(x, pltpu.VMEM)


def nt_dot(a, b):
    return lax.dot_general(a, b, (((1,), (1,)), ((), ())), preferred_element_type=F32)


def pick_kernel(send_hbm, init_hbm, hist_hbm, weight_hbm, out_ref, pack_a, pack_b, send_ref, chosen_ref, source_ref, weight_ref, sems):
    slots, peers = send_hbm.shape
    width, rows = init_hbm.shape
    layers = hist_hbm.shape[0] + 1
    copies = [pltpu.make_async_copy(init_hbm, source_ref.at[pl.ds(0, width), :], sems.at[0])]
    copies.append(pltpu.make_async_copy(weight_hbm, weight_ref, sems.at[1]))
    for k in range(layers - 1):
        place = source_ref.at[pl.ds((k + 1) * width, width), :]
        copies.append(pltpu.make_async_copy(hist_hbm.at[k], place, sems.at[k + 2]))
    lists_copy = pltpu.make_async_copy(send_hbm, send_ref, sems.at[layers + 1])
    lists_copy.start()
    for copy in copies:
        copy.start()
    lists_copy.wait()
    lists = send_ref[...].T
    spread = jnp.broadcast_to(lists[:, None, :], (peers, slots, slots)).reshape(peers * slots, slots)
    at = lax.broadcasted_iota(jnp.int32, spread.shape, 0) % slots
    lane = lax.broadcasted_iota(jnp.int32, spread.shape, 1)
    index = jnp.sum(jnp.where(at == lane, spread, 0), axis=1, keepdims=True)
    step = 64
    for begin in range(0, peers * slots, step):
        node = lax.broadcasted_iota(jnp.int32, (step, rows), 1)
        chosen_ref[begin : begin + step, :] = jnp.where(node == index[begin : begin + step], 1.0, 0.0).astype(BF)
    spare = out_ref.shape[1] - layers * width
    out_ref[:, layers * width :] = jnp.zeros((peers * slots, spare), BF)
    full = weight_ref.shape[2]
    parts = rows // full
    copies[1].wait()
    flat = weight_ref[...].reshape(-1, full)
    half = flat.shape[0] // 2
    for n, pack_ref in enumerate((pack_a, pack_b)):
        pack_ref[parts // 2 * width :, :] = flat[n * half : (n + 1) * half]
    copies[0].wait()
    for n, pack_ref in enumerate((pack_a, pack_b)):
        for j in range(parts // 2):
            begin = (n * parts // 2 + j) * full
            pack_ref[j * width : (j + 1) * width, :] = source_ref[:width, begin : begin + full]
    for copy in copies[2:]:
        copy.wait()
    out_ref[:, : layers * width] = nt_dot(chosen_ref[...], source_ref[...]).astype(BF)


def compact_kernel(got_ref, near_ref, far_ref, whole_ref):
    halo = got_ref.shape[0]
    half = halo // 2
    near_ref[:, :64] = got_ref[:half, :64]
    near_ref[:, 64:] = got_ref[half:, :64]
    far = got_ref[:, 64:192]
    far_ref[...] = far
    whole_ref[:half, :64] = got_ref[:half, :64]
    whole_ref[:half, 64:] = got_ref[half:, :64]
    whole_ref[half:, :] = far


def prep_kernel(mask_ref, adj_ref, far_ref, _, __, ___, masked_ref, scale_ref, later_ref):
    later_ref[...] = far_ref[...]
    rows, cols = masked_ref.shape
    step = 16
    for i in range(rows // TILE):
        keep = [jnp.full((1, TILE), mask_ref[i, t].astype(F32), F32) for t in range(cols // TILE)]
        keep = jnp.concatenate(keep, axis=1).astype(BF)
        for begin in range(i * TILE, (i + 1) * TILE, step):
            part = pl.ds(begin, step)
            held = adj_ref[part, :] * keep
            masked_ref[part, :] = held
            wide = held.astype(F32)
            total = wide[:, :TILE]
            for t in range(1, cols // TILE):
                total = total + wide[:, t * TILE : (t + 1) * TILE]
            scale = 0.9 / (1.0 + jnp.sum(total, axis=1, keepdims=True))
            scale_ref[part, :] = jnp.broadcast_to(scale, (step, scale_ref.shape[1]))


def own_kernel(place_ref, masked_ref, a0, a1, a2, a3, b0, b1, b2, b3, sums_ref, rest_ref, weight_ref, init_ref):
    rows = masked_ref.shape[0]
    full = init_ref.shape[1]
    width = full // 4
    parts = rows // full
    packs = ((a0, a1, a2, a3), (b0, b1, b2, b3))
    turned = lax.broadcasted_iota(jnp.int32, (full, full), 1) + width * place_ref[0]
    turned = jnp.where(turned >= full, turned - full, turned)
    turn = jnp.where(lax.broadcasted_iota(jnp.int32, (full, full), 0) == turned, 1.0, 0.0).astype(BF)
    for n, group in enumerate(packs):
        for j in range(parts // 2):
            piece = jnp.concatenate([pack[j * width : (j + 1) * width, :] for pack in group], axis=0)
            begin = (n * parts // 2 + j) * full
            init_ref[begin : begin + full, :] = piece.T
    begin = parts // 2 * width
    layers = weight_ref.shape[0]
    for k in range(4):
        flat = jnp.concatenate([group[k][begin:, :] for group in packs], axis=0)
        flat = jnp.dot(flat, turn, preferred_element_type=F32).astype(BF)
        for depth in range(layers):
            weight_ref[depth, k * width : (k + 1) * width, :] = flat[depth * width : (depth + 1) * width]
    block = 1024
    for begin in range(0, rows, block):
        part = pl.ds(begin, block)
        sums_ref[part, :] = jnp.dot(masked_ref[part, :rows], init_ref[...], preferred_element_type=F32)
    rest_ref[...] = 0.1 * init_ref[...].astype(F32)


def finish(depth, acc_ref, scale_ref, rest_ref, weight_ref, made_ref, send=None):
    step = 256
    beta = math.log(0.5 / (depth + 1) + 1.0)
    for begin in range(0, acc_ref.shape[0], step):
        part = pl.ds(begin, step)
        scale = jnp.concatenate([scale_ref[part, :]] * 2, axis=1)
        support = acc_ref[part, :] * scale + rest_ref[part, :]
        low = support.astype(BF)
        if depth == 2:
            product = jnp.dot(low, weight_ref[depth, :, :128], preferred_element_type=F32)
            made = jnp.maximum((1.0 - beta) * support[:, :128] + beta * product, 0.0)
            made_ref[:, part] = made.T[:64].astype(BF)
            send(begin // step).start()
        else:
            product = jnp.dot(low, weight_ref[depth], preferred_element_type=F32)
            made = jnp.maximum((1.0 - beta) * support + beta * product, 0.0).astype(BF)
            made_ref[part, :] = made


def early_kernel(masked_ref, scale_ref, sums_ref, rest_ref, weight_ref, b0, b1, b2, b3, next_ref, border, made, acc_ref):
    rows, cols = masked_ref.shape
    half = b2.shape[0]
    packs = [pack[:half, :] for pack in (b0, b1, b2, b3)]
    block = 1024
    border[:half, :] = jnp.concatenate([pack[:, :64] for pack in packs], axis=1)
    border[half:, :] = jnp.concatenate([pack[:, 64:] for pack in packs], axis=1)
    for begin in range(0, rows, block):
        whole = pl.ds(begin, block)
        more = jnp.dot(masked_ref[whole, rows:], border[...], preferred_element_type=F32)
        acc_ref[whole, :] = sums_ref[whole, :] + more
    finish(0, acc_ref, scale_ref, rest_ref, weight_ref, made)
    for begin in range(0, rows, block):
        whole = pl.ds(begin, block)
        next_ref[whole, :] = jnp.dot(masked_ref[whole, :rows], made[...], preferred_element_type=F32)


def late_kernel(masked_ref, scale_ref, sums_ref, rest_ref, weight_ref, b0, b1, b2, b3, out_hbm, joined, acc_ref, out_ref, sems):
    rows, cols = masked_ref.shape
    half = (cols - rows) // 2
    packs = (b0[half:, :], b1[half:, :], b2[...], b3[half:, :])
    block = 1024
    border = jnp.concatenate([pack[:, :64] for pack in packs], axis=1)
    joined[rows:, :] = jnp.concatenate([pack[:, 64:] for pack in packs], axis=1)
    for begin in range(0, rows, block):
        whole = pl.ds(begin, block)
        more = jnp.dot(masked_ref[whole, rows:], border, preferred_element_type=F32)
        acc_ref[whole, :] = sums_ref[whole, :] + more
    finish(1, acc_ref, scale_ref, rest_ref, weight_ref, joined)
    for begin in range(0, rows, block):
        whole = pl.ds(begin, block)
        acc_ref[whole, :] = jnp.dot(masked_ref[whole, :], joined[...], preferred_element_type=F32)
    count = sems.shape[0]
    size = rows // count

    def send(i):
        part = pl.ds(i * size, size)
        return pltpu.make_async_copy(out_ref.at[:, part], out_hbm.at[:, part], sems.at[i])

    finish(2, acc_ref, scale_ref, rest_ref, weight_ref, out_ref, send)
    for i in range(count):
        send(i).wait()


def ring(x, shift):
    return lax.ppermute(x, "feat", [((i + shift) % 4, i) for i in range(4)])


def local(initial, history, adjacency, tile_mask, send_lists, weights):
    rows, width = initial.shape
    peers, slots = send_lists.shape[1:]
    halo = peers * slots
    cols = rows + halo
    full = weights.shape[2]
    vmem = pl.BlockSpec(memory_space=pltpu.VMEM)
    smem = pl.BlockSpec(memory_space=pltpu.SMEM)
    hbm = pl.BlockSpec(memory_space=pltpu.HBM)
    params = pltpu.CompilerParams
    place = lax.axis_index("feat").astype(jnp.int32).reshape(1)
    layers = weights.shape[0]

    def in_hbm(x):
        return pltpu.with_memory_space_constraint(x, pltpu.HBM)

    outgoing, pack_a, pack_b = pl.pallas_call(
        pick_kernel,
        out_shape=[pltpu.VMEM((halo, full), BF)] + [pltpu.VMEM(((rows // full + layers) * width // 2, full), BF)] * 2,
        in_specs=[hbm] * 4,
        out_specs=[vmem] * 3,
        scratch_shapes=[
            pltpu.VMEM((slots, peers), jnp.int32),
            pltpu.VMEM((halo, rows), BF),
            pltpu.VMEM((layers * width, rows), BF),
            pltpu.VMEM(weights.shape, BF),
            pltpu.SemaphoreType.DMA((layers + 2,)),
        ],
        compiler_params=params(vmem_limit_bytes=8 * MIB),
        name="pick",
    )(in_hbm(send_lists[0].T), in_hbm(initial.T), in_hbm(jnp.swapaxes(history, 1, 2)), in_hbm(weights))
    a1, a3 = ring(pack_a, 1), ring(pack_a, 3)
    b1, b3 = ring(pack_b, 1), ring(pack_b, 3)
    packs = [pack_a, a1, ring(a1, 1), a3, pack_b, b1, ring(b3, 3), b3]

    arrived = lax.all_to_all(outgoing.reshape(peers, slots, full), "dom", split_axis=0, concat_axis=0, tiled=True)
    near, far, whole = pl.pallas_call(
        compact_kernel,
        out_shape=[pltpu.VMEM((size, 128), BF) for size in (halo // 2, halo, halo + halo // 2)],
        in_specs=[vmem],
        out_specs=[vmem] * 3,
        compiler_params=params(vmem_limit_bytes=2 * MIB),
        cost_estimate=pl.CostEstimate(flops=15000000000, bytes_accessed=1000, transcendentals=0),
        name="compact",
    )(in_vmem(arrived.reshape(halo, full)))
    after_all, before_all = ring(whole, 1), ring(whole, 3)
    nears = [whole, after_all, ring(near, 2), before_all]

    masked, scale, later = pl.pallas_call(
        prep_kernel,
        out_shape=[pltpu.VMEM((rows, cols), BF), pltpu.VMEM((rows, 128), F32), pltpu.VMEM((halo, 128), BF)],
        in_specs=[smem] + [vmem] * 5,
        out_specs=[vmem] * 3,
        compiler_params=params(vmem_limit_bytes=14 * MIB),
        cost_estimate=pl.CostEstimate(flops=4300001000, bytes_accessed=1000, transcendentals=0),
        name="prep",
    )(tile_mask, adjacency, in_vmem(far), *[in_vmem(packs[k]) for k in (2, 3, 5)])

    fars = [whole, after_all, ring(later, 2), before_all]
    sums, rest, turned = pl.pallas_call(
        own_kernel,
        out_shape=[
            pltpu.VMEM((rows, full), F32),
            pltpu.VMEM((rows, full), F32),
            pltpu.VMEM((layers, full, full), BF),
        ],
        in_specs=[smem] + [vmem] * 9,
        out_specs=[vmem] * 3,
        scratch_shapes=[pltpu.VMEM((rows, full), BF)],
        compiler_params=params(vmem_limit_bytes=8 * MIB),
        cost_estimate=pl.CostEstimate(flops=2100001000, bytes_accessed=1000, transcendentals=0),
        name="own",
    )(place, in_vmem(masked), *[in_vmem(p) for p in packs])

    sums = pl.pallas_call(
        early_kernel,
        out_shape=pltpu.VMEM((rows, full), F32),
        in_specs=[vmem] * 9,
        out_specs=vmem,
        scratch_shapes=[pltpu.VMEM((halo, full), BF), pltpu.VMEM((rows, full), BF), pltpu.VMEM((rows, full), F32)],
        compiler_params=params(vmem_limit_bytes=10 * MIB),
        cost_estimate=pl.CostEstimate(flops=1000, bytes_accessed=1000, transcendentals=0),
        name="early",
    )(*[in_vmem(x) for x in (masked, scale, sums, rest, turned, *nears)])

    out = pl.pallas_call(
        late_kernel,
        out_shape=jax.ShapeDtypeStruct((width, rows), BF),
        in_specs=[vmem] * 9,
        out_specs=hbm,
        scratch_shapes=[
            pltpu.VMEM((cols, full), BF),
            pltpu.VMEM((rows, full), F32),
            pltpu.VMEM((width, rows), BF),
            pltpu.SemaphoreType.DMA((rows // 256,)),
        ],
        compiler_params=params(vmem_limit_bytes=10 * MIB),
        name="late",
    )(*[in_vmem(x) for x in (masked, scale, sums, rest, turned, *fars)])
    return out.T


def solution(mesh):
    placed = (
        P("dom", "feat"),
        P(None, "dom", "feat"),
        P("dom", None),
        P("dom", None),
        P("dom", None, None),
        P(None, "feat", None),
    )
    return jax.shard_map(
        local, mesh=mesh, in_specs=placed, out_specs=P("dom", "feat"), check_vma=False
    )
```

```python
import functools
import math

import jax
import jax.numpy as jnp
from jax import lax
from jax.experimental import pallas as pl
from jax.experimental.pallas import tpu as pltpu
from jax.sharding import PartitionSpec as P

TILE = 128
BF = jnp.bfloat16
F32 = jnp.float32
MIB = 2**20


def in_vmem(x):
    return pltpu.with_memory_space_constraint(x, pltpu.VMEM)


def nt_dot(a, b):
    return lax.dot_general(a, b, (((1,), (1,)), ((), ())), preferred_element_type=F32)


def pick_kernel(send_hbm, init_hbm, hist_hbm, weight_hbm, out_ref, pack_a, pack_b, send_ref, chosen_ref, source_ref, weight_ref, sems):
    slots, peers = send_hbm.shape
    width, rows = init_hbm.shape
    layers = hist_hbm.shape[0] + 1
    copies = [pltpu.make_async_copy(init_hbm, source_ref.at[pl.ds(0, width), :], sems.at[0])]
    copies.append(pltpu.make_async_copy(weight_hbm, weight_ref, sems.at[1]))
    for k in range(layers - 1):
        place = source_ref.at[pl.ds((k + 1) * width, width), :]
        copies.append(pltpu.make_async_copy(hist_hbm.at[k], place, sems.at[k + 2]))
    lists_copy = pltpu.make_async_copy(send_hbm, send_ref, sems.at[layers + 1])
    lists_copy.start()
    for copy in copies:
        copy.start()
    lists_copy.wait()
    lists = send_ref[...].T
    spread = jnp.broadcast_to(lists[:, None, :], (peers, slots, slots)).reshape(peers * slots, slots)
    at = lax.broadcasted_iota(jnp.int32, spread.shape, 0) % slots
    lane = lax.broadcasted_iota(jnp.int32, spread.shape, 1)
    index = jnp.sum(jnp.where(at == lane, spread, 0), axis=1, keepdims=True)
    step = 64
    for begin in range(0, peers * slots, step):
        node = lax.broadcasted_iota(jnp.int32, (step, rows), 1)
        chosen_ref[begin : begin + step, :] = jnp.where(node == index[begin : begin + step], 1.0, 0.0).astype(BF)
    spare = out_ref.shape[1] - layers * width
    out_ref[:, layers * width :] = jnp.zeros((peers * slots, spare), BF)
    full = weight_ref.shape[2]
    parts = rows // full
    copies[1].wait()
    flat = weight_ref[...].reshape(-1, full)
    half = flat.shape[0] // 2
    for n, pack_ref in enumerate((pack_a, pack_b)):
        pack_ref[parts // 2 * width :, :] = flat[n * half : (n + 1) * half]
    copies[0].wait()
    for n, pack_ref in enumerate((pack_a, pack_b)):
        for j in range(parts // 2):
            begin = (n * parts // 2 + j) * full
            pack_ref[j * width : (j + 1) * width, :] = source_ref[:width, begin : begin + full]
    for copy in copies[2:]:
        copy.wait()
    out_ref[:, : layers * width] = nt_dot(chosen_ref[...], source_ref[...]).astype(BF)


def compact_kernel(got_ref, near_ref, far_ref, whole_ref):
    halo = got_ref.shape[0]
    half = halo // 2
    near_ref[:, :64] = got_ref[:half, :64]
    near_ref[:, 64:] = got_ref[half:, :64]
    far = got_ref[:, 64:192]
    far_ref[...] = far
    whole_ref[:half, :64] = got_ref[:half, :64]
    whole_ref[:half, 64:] = got_ref[half:, :64]
    whole_ref[half:, :] = far


def prep_kernel(mask_ref, adj_ref, far_ref, _, __, ___, masked_ref, scale_ref, later_ref):
    later_ref[...] = far_ref[...]
    rows, cols = masked_ref.shape
    step = 32
    for i in range(rows // TILE):
        keep = [jnp.full((1, TILE), mask_ref[i, t].astype(F32), F32) for t in range(cols // TILE)]
        keep = jnp.concatenate(keep, axis=1).astype(BF)
        for begin in range(i * TILE, (i + 1) * TILE, step):
            part = pl.ds(begin, step)
            held = adj_ref[part, :] * keep
            masked_ref[part, :] = held
            wide = held.astype(F32)
            total = wide[:, :TILE]
            for t in range(1, cols // TILE):
                total = total + wide[:, t * TILE : (t + 1) * TILE]
            scale = 0.9 / (1.0 + jnp.sum(total, axis=1, keepdims=True))
            scale_ref[part, :] = jnp.broadcast_to(scale, (step, scale_ref.shape[1]))


def own_kernel(place_ref, masked_ref, a0, a1, a2, a3, b0, b1, b2, b3, sums_ref, rest_ref, weight_ref, init_ref):
    rows = masked_ref.shape[0]
    full = init_ref.shape[1]
    width = full // 4
    parts = rows // full
    packs = ((a0, a1, a2, a3), (b0, b1, b2, b3))
    turned = lax.broadcasted_iota(jnp.int32, (full, full), 1) + width * place_ref[0]
    turned = jnp.where(turned >= full, turned - full, turned)
    turn = jnp.where(lax.broadcasted_iota(jnp.int32, (full, full), 0) == turned, 1.0, 0.0).astype(BF)
    for n, group in enumerate(packs):
        for j in range(parts // 2):
            piece = jnp.concatenate([pack[j * width : (j + 1) * width, :] for pack in group], axis=0)
            begin = (n * parts // 2 + j) * full
            init_ref[begin : begin + full, :] = piece.T
    begin = parts // 2 * width
    layers = weight_ref.shape[0]
    for k in range(4):
        flat = jnp.concatenate([group[k][begin:, :] for group in packs], axis=0)
        flat = jnp.dot(flat, turn, preferred_element_type=F32).astype(BF)
        for depth in range(layers):
            weight_ref[depth, k * width : (k + 1) * width, :] = flat[depth * width : (depth + 1) * width]
    block = 1024
    for begin in range(0, rows, block):
        part = pl.ds(begin, block)
        sums_ref[part, :] = jnp.dot(masked_ref[part, :rows], init_ref[...], preferred_element_type=F32)
    rest_ref[...] = 0.1 * init_ref[...].astype(F32)


def finish(depth, acc_ref, scale_ref, rest_ref, weight_ref, made_ref):
    step = 256
    beta = math.log(0.5 / (depth + 1) + 1.0)
    for begin in range(0, acc_ref.shape[0], step):
        part = pl.ds(begin, step)
        scale = jnp.concatenate([scale_ref[part, :]] * 2, axis=1)
        support = acc_ref[part, :] * scale + rest_ref[part, :]
        low = support.astype(BF)
        if depth == 2:
            product = jnp.dot(low, weight_ref[depth, :, :128], preferred_element_type=F32)
            made = jnp.maximum((1.0 - beta) * support[:, :128] + beta * product, 0.0)
            made_ref[:, part] = made.T[:64].astype(BF)
        else:
            product = jnp.dot(low, weight_ref[depth], preferred_element_type=F32)
            made = jnp.maximum((1.0 - beta) * support + beta * product, 0.0).astype(BF)
            made_ref[part, :] = made


def early_kernel(masked_ref, scale_ref, sums_ref, rest_ref, weight_ref, b0, b1, b2, b3, next_ref, border, made, acc_ref):
    rows, cols = masked_ref.shape
    half = b2.shape[0]
    packs = [pack[:half, :] for pack in (b0, b1, b2, b3)]
    block = 1024
    border[:half, :] = jnp.concatenate([pack[:, :64] for pack in packs], axis=1)
    border[half:, :] = jnp.concatenate([pack[:, 64:] for pack in packs], axis=1)
    for begin in range(0, rows, block):
        whole = pl.ds(begin, block)
        more = jnp.dot(masked_ref[whole, rows:], border[...], preferred_element_type=F32)
        acc_ref[whole, :] = sums_ref[whole, :] + more
    finish(0, acc_ref, scale_ref, rest_ref, weight_ref, made)
    for begin in range(0, rows, block):
        whole = pl.ds(begin, block)
        next_ref[whole, :] = jnp.dot(masked_ref[whole, :rows], made[...], preferred_element_type=F32)


def late_kernel(masked_ref, scale_ref, sums_ref, rest_ref, weight_ref, b0, b1, b2, b3, out_ref, joined, acc_ref):
    rows, cols = masked_ref.shape
    half = (cols - rows) // 2
    packs = (b0[half:, :], b1[half:, :], b2[...], b3[half:, :])
    block = 1024
    border = jnp.concatenate([pack[:, :64] for pack in packs], axis=1)
    joined[rows:, :] = jnp.concatenate([pack[:, 64:] for pack in packs], axis=1)
    for begin in range(0, rows, block):
        whole = pl.ds(begin, block)
        more = jnp.dot(masked_ref[whole, rows:], border, preferred_element_type=F32)
        acc_ref[whole, :] = sums_ref[whole, :] + more
    finish(1, acc_ref, scale_ref, rest_ref, weight_ref, joined)
    for begin in range(0, rows, block):
        whole = pl.ds(begin, block)
        acc_ref[whole, :] = jnp.dot(masked_ref[whole, :], joined[...], preferred_element_type=F32)
    finish(2, acc_ref, scale_ref, rest_ref, weight_ref, out_ref)


def ring(x, shift):
    return lax.ppermute(x, "feat", [((i + shift) % 4, i) for i in range(4)])


def local(initial, history, adjacency, tile_mask, send_lists, weights):
    rows, width = initial.shape
    peers, slots = send_lists.shape[1:]
    halo = peers * slots
    cols = rows + halo
    full = weights.shape[2]
    vmem = pl.BlockSpec(memory_space=pltpu.VMEM)
    smem = pl.BlockSpec(memory_space=pltpu.SMEM)
    hbm = pl.BlockSpec(memory_space=pltpu.HBM)
    params = pltpu.CompilerParams
    place = lax.axis_index("feat").astype(jnp.int32).reshape(1)
    layers = weights.shape[0]

    def in_hbm(x):
        return pltpu.with_memory_space_constraint(x, pltpu.HBM)

    outgoing, pack_a, pack_b = pl.pallas_call(
        pick_kernel,
        out_shape=[pltpu.VMEM((halo, full), BF)] + [pltpu.VMEM(((rows // full + layers) * width // 2, full), BF)] * 2,
        in_specs=[hbm] * 4,
        out_specs=[vmem] * 3,
        scratch_shapes=[
            pltpu.VMEM((slots, peers), jnp.int32),
            pltpu.VMEM((halo, rows), BF),
            pltpu.VMEM((layers * width, rows), BF),
            pltpu.VMEM(weights.shape, BF),
            pltpu.SemaphoreType.DMA((layers + 2,)),
        ],
        compiler_params=params(vmem_limit_bytes=8 * MIB),
        name="pick",
    )(in_hbm(send_lists[0].T), in_hbm(initial.T), in_hbm(jnp.swapaxes(history, 1, 2)), in_hbm(weights))
    a1, a3 = ring(pack_a, 1), ring(pack_a, 3)
    b1, b3 = ring(pack_b, 1), ring(pack_b, 3)
    packs = [pack_a, a1, ring(a1, 1), a3, pack_b, b1, ring(b3, 3), b3]

    arrived = lax.all_to_all(outgoing.reshape(peers, slots, full), "dom", split_axis=0, concat_axis=0, tiled=True)
    near, far, whole = pl.pallas_call(
        compact_kernel,
        out_shape=[pltpu.VMEM((size, 128), BF) for size in (halo // 2, halo, halo + halo // 2)],
        in_specs=[vmem],
        out_specs=[vmem] * 3,
        compiler_params=params(vmem_limit_bytes=2 * MIB),
        cost_estimate=pl.CostEstimate(flops=15000000000, bytes_accessed=1000, transcendentals=0),
        name="compact",
    )(in_vmem(arrived.reshape(halo, full)))
    after_all, before_all = ring(whole, 1), ring(whole, 3)
    nears = [whole, after_all, ring(near, 2), before_all]

    masked, scale, later = pl.pallas_call(
        prep_kernel,
        out_shape=[pltpu.VMEM((rows, cols), BF), pltpu.VMEM((rows, 128), F32), pltpu.VMEM((halo, 128), BF)],
        in_specs=[smem] + [vmem] * 5,
        out_specs=[vmem] * 3,
        compiler_params=params(vmem_limit_bytes=14 * MIB),
        cost_estimate=pl.CostEstimate(flops=4300001000, bytes_accessed=1000, transcendentals=0),
        name="prep",
    )(tile_mask, adjacency, in_vmem(far), *[in_vmem(packs[k]) for k in (2, 3, 5)])

    fars = [whole, after_all, ring(later, 2), before_all]
    sums, rest, turned = pl.pallas_call(
        own_kernel,
        out_shape=[
            pltpu.VMEM((rows, full), F32),
            pltpu.VMEM((rows, full), F32),
            pltpu.VMEM((layers, full, full), BF),
        ],
        in_specs=[smem] + [vmem] * 9,
        out_specs=[vmem] * 3,
        scratch_shapes=[pltpu.VMEM((rows, full), BF)],
        compiler_params=params(vmem_limit_bytes=8 * MIB),
        cost_estimate=pl.CostEstimate(flops=2100001000, bytes_accessed=1000, transcendentals=0),
        name="own",
    )(place, in_vmem(masked), *[in_vmem(p) for p in packs])

    sums = pl.pallas_call(
        early_kernel,
        out_shape=pltpu.VMEM((rows, full), F32),
        in_specs=[vmem] * 9,
        out_specs=vmem,
        scratch_shapes=[pltpu.VMEM((halo, full), BF), pltpu.VMEM((rows, full), BF), pltpu.VMEM((rows, full), F32)],
        compiler_params=params(vmem_limit_bytes=10 * MIB),
        cost_estimate=pl.CostEstimate(flops=1000, bytes_accessed=1000, transcendentals=0),
        name="early",
    )(*[in_vmem(x) for x in (masked, scale, sums, rest, turned, *nears)])

    out = pl.pallas_call(
        late_kernel,
        out_shape=jax.ShapeDtypeStruct((width, rows), BF),
        in_specs=[vmem] * 9,
        out_specs=vmem,
        scratch_shapes=[pltpu.VMEM((cols, full), BF), pltpu.VMEM((rows, full), F32)],
        compiler_params=params(vmem_limit_bytes=10 * MIB),
        name="late",
    )(*[in_vmem(x) for x in (masked, scale, sums, rest, turned, *fars)])
    return out.T


def solution(mesh):
    placed = (
        P("dom", "feat"),
        P(None, "dom", "feat"),
        P("dom", None),
        P("dom", None),
        P("dom", None, None),
        P(None, "feat", None),
    )
    return jax.shard_map(
        local, mesh=mesh, in_specs=placed, out_specs=P("dom", "feat"), check_vma=False
    )
```
